256 devices in a mesh: pipe: 4 (over z_lo, core), fsdp: 64 (over x, z_hi, y).
Axes of the slice: x: 4, y: 4, z: 8 (z_hi: 4, z_lo: 2; z = z_hi * 2 + z_lo), core: 2. Of those that a mesh axis runs over, the one named last changes fastest.
Arguments:
- tokens: int32 [2, 160], replicated, may hold values from 0 to 511
- embed: bfloat16 [512, 8192], P(None, 'fsdp'), may hold values from -60 to 60
- gain: bfloat16 [4, 8192], P('pipe', 'fsdp'), may hold values from 0.099609375 to 1.8984375
- w_in: bfloat16 [4, 3, 8192, 8192], P('pipe', None, None, 'fsdp'), may hold values from -0.0625 to 0.0625
- short_filter: float32 [4, 3, 7, 8192], P('pipe', None, None, 'fsdp'), may hold values from -2 to 2
- long_filter: float32 [4, 512, 128], P('pipe', 'fsdp'), may hold values from -0.5 to 0.5
- skip_bias: float32 [4, 8192], P('pipe', 'fsdp'), may hold values from -1 to 1
- w_out: bfloat16 [4, 8192, 8192], P('pipe', None, 'fsdp'), may hold values from -0.0625 to 0.0625
Outputs:
- hidden: bfloat16 [2, 160, 8192], P(None, 'pipe', 'fsdp')
The draws below stay inside these ranges and needn't reach their ends.
All inputs are finite; a program needn't handle non-finite values.
Results may differ from the reference program's by a relative error of at most 0.035.
Values may be sent and summed in bfloat16 or wider, within the bound.
No kernel may reach another device: no remote copies, remote signals or barrier semaphores. Data moves between devices by JAX's collectives and lax.ppermute only.
A program may use at most 64 MiB of HBM per device.

```python
import jax
import jax.numpy as jnp
from jax import lax

D = 8192
VOCAB = 512
GROUP = 16
LTAPS = 128
STAPS = 7
SEQ = 160
MB = 2
LAYERS = 4
FILTERS = 512


def draw_embed(key, part):
    key = jax.random.fold_in(key, 11)
    key_base, key_rows, key_cols = jax.random.split(key, 3)
    rising = 3.0 ** (jnp.arange(D, dtype=jnp.float32) / (D - 1))
    base = jnp.clip(jax.random.normal(key_base, (VOCAB, D), jnp.float32), -4.0, 4.0)
    row_scale = jnp.exp(jax.random.uniform(key_rows, (VOCAB, 1), jnp.float32) * jnp.log(10.0))
    col_scale = jnp.exp(jax.random.uniform(key_cols, (1, D), jnp.float32) * jnp.log(2.0)) * rising[None, :]
    return (0.25 * base * row_scale * col_scale).astype(jnp.bfloat16)


def with_ends(entries, own_key, low, top_value):
    longest = entries.shape.index(max(entries.shape))
    spots = []
    for shift in (0, 1):
        where = [jax.random.randint(jax.random.fold_in(own_key, axis), (), 0, length) for axis, length in enumerate(entries.shape)]
        where[longest] = (where[longest] + shift) % entries.shape[longest]
        spots.append(tuple(where))
    return entries.at[spots[0]].set(low).at[spots[1]].set(top_value)


def block_scale(stream_key, shape, cuts, smallest, largest):
    level, own = 1.0, jax.random.fold_in(stream_key, 6)
    for axis_at, parts in cuts:
        heights = jnp.exp(jax.random.uniform(jax.random.fold_in(own, axis_at), (parts,), jnp.float32, smallest / len(cuts), largest / len(cuts)))
        level = level * jnp.repeat(heights, shape[axis_at] // parts).reshape([-1 if axis == axis_at else 1 for axis in range(len(shape))])
    return level


def scatter_about(stream_key, shape, deviation, most, pieces=(), kind=jnp.bfloat16):
    drawn = jax.random.normal(stream_key, shape, jnp.float32) * deviation
    if len(pieces) > 0:
        drawn = block_scale(stream_key, shape, pieces, -0.22, 0.18) * drawn
    return jnp.clip(drawn, min=-most, max=most).astype(kind)


def setup_inputs(seed: int = 0) -> dict:
    arg_keys = jax.random.split(jax.random.key(seed), 9)
    tokens = with_ends(jax.random.randint(arg_keys[0], (MB, SEQ), 0, VOCAB), jax.random.fold_in(arg_keys[0], 1), 0, VOCAB - 1).astype(jnp.int32)
    embed = draw_embed(jax.random.fold_in(arg_keys[8], 71), 0)
    gain = jnp.clip(1.0 + 0.18 * jax.random.normal(arg_keys[2], (LAYERS, D), jnp.float32), 0.099609375, 1.8984375).astype(jnp.bfloat16)
    w_in = scatter_about(arg_keys[3], (LAYERS, 3, D, D), D ** -0.5, 0.0625, ((0, 4), (3, 64)))
    short_filter = scatter_about(arg_keys[4], (LAYERS, 3, STAPS, D), STAPS ** -0.5, 2.0, ((0, 4), (3, 64)), jnp.float32)
    long_filter = scatter_about(arg_keys[5], (LAYERS, FILTERS, LTAPS), LTAPS ** -0.5, 0.5, ((0, 4), (1, 64)), jnp.float32)
    skip_bias = jnp.clip(jax.random.uniform(arg_keys[6], (LAYERS, D), jnp.float32, -1.0, 1.0) * block_scale(arg_keys[6], (LAYERS, D), ((0, 4), (1, 64)), -0.4, 0.0), -1.0, 1.0)
    w_out = scatter_about(arg_keys[7], (LAYERS, D, D), D ** -0.5, 0.0625, ((0, 4), (2, 64)))
    return dict(tokens=tokens, embed=embed, gain=gain, w_in=w_in, short_filter=short_filter, long_filter=long_filter, skip_bias=skip_bias, w_out=w_out)


def short_mix(projected, filters):
    width = filters.shape[1]
    seq_len = projected.shape[1]
    padded = jnp.pad(projected.astype(jnp.float32), ((0, 0), (width - 1, 0), (0, 0)))
    running = jnp.zeros(projected.shape, jnp.float32)
    for offset in range(width):
        window = padded[:, width - 1 - offset:width - 1 - offset + seq_len, :]
        running = running + filters[:, offset][:, None, :] * window
    return running

def long_mix(signal, kernels, group_size):
    seq_len = signal.shape[0]
    span = kernels.shape[1]
    count_filters = kernels.shape[0]
    positions = jnp.arange(seq_len, dtype=jnp.int32)
    lag_table = positions[:, None] - positions[None, :]
    inside = (lag_table >= 0) & (lag_table < span)
    lag_index = jnp.clip(lag_table, 0, span - 1)
    toeplitz = jnp.where(inside[None, :, :], kernels[:, lag_index], jnp.float32(0.0))
    grouped = signal.reshape(seq_len, count_filters, group_size)
    mixed = jnp.einsum('fts,sfg->tfg', toeplitz, grouped, precision=lax.Precision.HIGHEST)
    return mixed.reshape(seq_len, count_filters * group_size)

def layer_step(activation, gain_row, in_weights, short_taps, long_taps, skip_row, out_weight):
    widened = activation.astype(jnp.float32)
    mean_square = lax.optimization_barrier(jnp.mean(widened * widened, axis=1, keepdims=True))
    normalized = (widened * lax.rsqrt(mean_square + 1e-06) * gain_row.astype(jnp.float32)).astype(jnp.bfloat16)
    projected = jnp.stack([jnp.dot(normalized, in_weights[index], preferred_element_type=jnp.float32) for index in range(3)]).astype(jnp.bfloat16)
    mixed = short_mix(projected, short_taps)
    product = mixed[1] * mixed[2]
    carried = long_mix(product, long_taps, GROUP) + skip_row[None, :] * product
    gated = (mixed[0] * carried).astype(jnp.bfloat16)
    return (widened + jnp.dot(gated, out_weight, preferred_element_type=jnp.float32)).astype(jnp.bfloat16)

def reference(tokens, embed, gain, w_in, short_filter, long_filter, skip_bias, w_out):
    results = []
    for micro_index in range(MB):
        activation = embed[tokens[micro_index]]
        for layer_index in range(LAYERS):
            activation = layer_step(activation, gain[layer_index], w_in[layer_index], short_filter[layer_index], long_filter[layer_index], skip_bias[layer_index], w_out[layer_index])
        results.append(activation)
    return jnp.stack(results)
```

```python
import itertools

import jax
import jax.numpy as jnp
from jax import lax
from jax.experimental import pallas as pl
from jax.experimental.pallas import tpu as pltpu
from jax.sharding import PartitionSpec as P

D = 8192
STAPS = 7
SEQ = 160
LANES = 128
GROUP = 16
TABLE = 256
SIDE = 4
AXES = ("pipe", "fsdp")
PIPES = 4
FSDP = 64
EXTRA = 16
F32 = jnp.float32
BF16 = jnp.bfloat16


def place(x, z, y):
    return (x * SIDE + z) * SIDE + y


LINES_Z = [
    [p * FSDP + place(x, z, y) for z in range(SIDE)]
    for p, x, y in itertools.product(range(PIPES), range(SIDE), range(SIDE))
]
PLANES_XY = [
    [p * FSDP + place(x, z, y) for x, y in itertools.product(range(SIDE), range(SIDE))]
    for p, z in itertools.product(range(PIPES), range(SIDE))
]


def hop(value, moves):
    pairs = [(a * FSDP + f, b * FSDP + f) for a, b in moves for f in range(FSDP)]
    return lax.ppermute(value, AXES, pairs)


def share(value, groups):
    count = len(groups[0])
    copies = jnp.broadcast_to(value[None], (count,) + value.shape)
    return lax.all_to_all(copies, AXES, 0, 0, axis_index_groups=groups)


def gather_channels(block):
    return share(share(block, LINES_Z), PLANES_XY)


def toeplitz_kernel(base_ref, out_ref):
    row = lax.broadcasted_iota(jnp.int32, (SEQ, TABLE), 0)
    column = lax.broadcasted_iota(jnp.int32, (SEQ, TABLE), 1)
    for index in range(base_ref.shape[0]):
        base = jnp.broadcast_to(base_ref[index : index + 1, :], (SEQ, TABLE))
        turned = pltpu.roll(base, 0, 1, stride=1, stride_axis=0)
        out_ref[index] = jnp.where(column <= row, turned, 0.0).astype(BF16)


def toeplitz(long_taps):
    count = long_taps.shape[0]
    base = jnp.concatenate(
        [long_taps[:, :1], jnp.zeros((count, TABLE - LANES), F32), long_taps[:, :0:-1]], axis=1
    )
    return pl.pallas_call(
        toeplitz_kernel,
        out_shape=jax.ShapeDtypeStruct((count, SEQ, TABLE), BF16),
        name="toeplitz",
    )(base)


def mix_kernel(layer, x_ref, gain_ref, w_ref, taps_ref, toep_ref, out_ref, total, squares, padded):
    step = pl.program_id(0) * SIDE + pl.program_id(1)

    @pl.when(step == 0)
    def _():
        total[...] = jnp.zeros_like(total)
        squares[...] = jnp.zeros_like(squares)

    scaled = []
    power = squares[...]
    for z in range(SIDE):
        wide = x_ref[0, z].astype(F32)
        power = power + wide * wide
        gain = gain_ref[0, z].astype(F32)[layer : layer + 1, :]
        scaled.append((wide * gain).astype(BF16))
    squares[...] = power
    left = jnp.concatenate(scaled, axis=1)
    right = jnp.concatenate(
        [w_ref[0, j, 0, :, 0].reshape(SIDE * LANES, LANES) for j in range(3)], axis=1
    )
    total[...] += jnp.dot(left, right, preferred_element_type=F32)

    @pl.when(step == SIDE * SIDE - 1)
    def _():
        mean = jnp.sum(squares[...], axis=1, keepdims=True) / D
        inverse = lax.rsqrt(mean + 1e-06)
        mixed = []
        for j in range(3):
            projected = (total[:, j * LANES : (j + 1) * LANES] * inverse).astype(BF16)
            padded[j, :EXTRA] = jnp.zeros((EXTRA, LANES), F32)
            padded[j, EXTRA:] = projected.astype(F32)
            running = jnp.zeros((SEQ, LANES), F32)
            for i in range(STAPS):
                tap = taps_ref[j * STAPS + i : j * STAPS + i + 1, :]
                running = running + tap * padded[j, EXTRA - i : EXTRA - i + SEQ, :]
            mixed.append(running)
        product = mixed[1] * mixed[2]
        carried = taps_ref[3 * STAPS : 3 * STAPS + 1, :] * product
        lane = lax.broadcasted_iota(jnp.int32, (TABLE, LANES), 1)
        tall = jnp.concatenate([product, jnp.zeros((TABLE - SEQ, LANES), F32)], axis=0)
        for f in range(LANES // GROUP):
            kept = jnp.where(lane // GROUP == f, tall, 0.0).astype(BF16)
            carried = carried + jnp.dot(toep_ref[0, f], kept, preferred_element_type=F32)
        out_ref[...] = (mixed[0] * carried).astype(BF16)


def mix(layer, gathered, gains, weights, taps, toep):
    def whole(shape, first=0):
        return pl.BlockSpec(shape, lambda x, y: (first,) + (0,) * (len(shape) - 1))

    def kernel(*refs):
        mix_kernel(layer, *refs)

    filters = LANES // GROUP
    return pl.pallas_call(
        kernel,
        grid=(SIDE, SIDE),
        in_specs=[
            pl.BlockSpec((1, SIDE, SEQ, LANES), lambda x, y: (x * SIDE + y, 0, 0, 0)),
            pl.BlockSpec((1, SIDE, EXTRA, LANES), lambda x, y: (x * SIDE + y, 0, 0, 0)),
            pl.BlockSpec(
                (1, 3, 1, SIDE, 1, LANES, LANES), lambda x, y: (layer, 0, x, 0, y, 0, 0)
            ),
            whole((3 * STAPS + 3, LANES)),
            whole((1, filters, SEQ, TABLE), layer),
        ],
        out_specs=whole((SEQ, LANES)),
        out_shape=jax.ShapeDtypeStruct((SEQ, LANES), BF16),
        scratch_shapes=[
            pltpu.VMEM((SEQ, 3 * LANES), F32),
            pltpu.VMEM((SEQ, LANES), F32),
            pltpu.VMEM((3, EXTRA + SEQ, LANES), F32),
        ],
        compiler_params=pltpu.CompilerParams(vmem_limit_bytes=24 << 20),
        name="mix",
    )(gathered, gains, weights, taps, toep)


def out_kernel(g_ref, w_ref, x_ref, out_ref, total):
    step = pl.program_id(0) * SIDE + pl.program_id(1)

    @pl.when(step == 0)
    def _():
        total[...] = x_ref[...].astype(F32)

    left = jnp.concatenate([g_ref[0, z] for z in range(SIDE)], axis=1)
    right = w_ref[0, 0, :, 0].reshape(SIDE * LANES, LANES)
    total[...] += jnp.dot(left, right, preferred_element_type=F32)

    @pl.when(step == SIDE * SIDE - 1)
    def _():
        out_ref[...] = total[...].astype(BF16)


def project_out(layer, gathered, weights, activation):
    return pl.pallas_call(
        out_kernel,
        grid=(SIDE, SIDE),
        in_specs=[
            pl.BlockSpec((1, SIDE, SEQ, LANES), lambda x, y: (x * SIDE + y, 0, 0, 0)),
            pl.BlockSpec((1, 1, SIDE, 1, LANES, LANES), lambda x, y: (layer, x, 0, y, 0, 0)),
            pl.BlockSpec((SEQ, LANES), lambda x, y: (0, 0)),
        ],
        out_specs=pl.BlockSpec((SEQ, LANES), lambda x, y: (0, 0)),
        out_shape=jax.ShapeDtypeStruct((SEQ, LANES), BF16),
        scratch_shapes=[pltpu.VMEM((SEQ, LANES), F32)],
        compiler_params=pltpu.CompilerParams(vmem_limit_bytes=24 << 20),
        name="project_out",
    )(gathered, weights, activation)


CORES = [[0, 1], [2, 3]]


def body(tokens, embed, gain, w_in, short_filter, long_filter, skip_bias, w_out):
    core = lax.axis_index("pipe") % 2
    swap = [(0, 1), (1, 0), (2, 3), (3, 2)]

    own = jnp.concatenate(
        [
            short_filter[0].reshape(3 * STAPS, LANES),
            skip_bias,
            gain.astype(F32),
            jnp.zeros((1, LANES), F32),
            long_filter[0],
        ],
        axis=0,
    )
    other = hop(own, swap)
    first, second = jnp.where(core == 0, own, other), jnp.where(core == 0, other, own)
    w_in_both = lax.all_gather(w_in[0], "pipe", axis_index_groups=CORES)
    w_out_both = lax.all_gather(w_out[0], "pipe", axis_index_groups=CORES)
    w_in_both = w_in_both.reshape(2, 3, SIDE, SIDE, SIDE, LANES, LANES)
    w_out_both = w_out_both.reshape(2, SIDE, SIDE, SIDE, LANES, LANES)
    rows = 3 * STAPS + 3
    taps = [first[:rows], second[:rows]]
    toep = toeplitz(jnp.concatenate([first[rows:], second[rows:]], axis=0))
    toep = toep.reshape(2, LANES // GROUP, SEQ, TABLE)

    ids = lax.dynamic_index_in_dim(tokens, core, 0, keepdims=False)
    one_hot = (ids[:, None] == jnp.arange(embed.shape[0], dtype=jnp.int32)[None, :]).astype(BF16)
    activation = jnp.dot(one_hot, embed, preferred_element_type=F32).astype(BF16)

    gain_rows = jnp.concatenate(
        [first[rows - 2 : rows - 1], second[rows - 2 : rows - 1], jnp.zeros((EXTRA - 2, LANES), F32)],
        axis=0,
    )
    arrived = gather_channels(jnp.concatenate([activation, gain_rows.astype(BF16)], axis=0))
    gathered, gains = arrived[:, :, :SEQ], arrived[:, :, SEQ:]
    for part in range(2):
        for layer in range(2):
            if part + layer > 0:
                gathered = gather_channels(activation)
            gated = mix(layer, gathered, gains, w_in_both, taps[layer], toep)
            activation = project_out(layer, gather_channels(gated), w_out_both, activation)
        if part == 0:
            activation = hop(activation, [(0, 2), (1, 3)])

    quarters = activation.reshape(4, SEQ // 4, LANES)
    even, odd = quarters[0::2], quarters[1::2]
    keep = jnp.where(core == 0, even, odd)
    taken = hop(jnp.where(core == 0, odd, even), swap)
    row_0, row_1 = jnp.where(core == 0, keep, taken), jnp.where(core == 0, taken, keep)
    low, high = jnp.stack([row_0[0], row_1[0]]), jnp.stack([row_0[1], row_1[1]])
    passed = hop(low, [(2, 0), (3, 1)])
    return jnp.where(lax.axis_index("pipe") < 2, passed, high)


def solution(mesh):
    return jax.shard_map(
        body,
        mesh=mesh,
        in_specs=(
            P(),
            P(None, "fsdp"),
            P("pipe", "fsdp"),
            P("pipe", None, None, "fsdp"),
            P("pipe", None, None, "fsdp"),
            P("pipe", "fsdp", None),
            P("pipe", "fsdp"),
            P("pipe", None, "fsdp"),
        ),
        out_specs=P(None, "pipe", "fsdp"),
        check_vma=False,
    )
```

```python
import itertools

import jax
import jax.numpy as jnp
from jax import lax
from jax.experimental import pallas as pl
from jax.experimental.pallas import tpu as pltpu
from jax.sharding import PartitionSpec as P

D = 8192
STAPS = 7
SEQ = 160
LANES = 128
GROUP = 16
TABLE = 256
SIDE = 4
AXES = ("pipe", "fsdp")
PIPES = 4
FSDP = 64
EXTRA = 16
VMEM_LIMIT = 48 << 20
F32 = jnp.float32
BF16 = jnp.bfloat16


def place(x, z, y):
    return (x * SIDE + z) * SIDE + y


LINES_Z = [
    [p * FSDP + place(x, z, y) for z in range(SIDE)]
    for p, x, y in itertools.product(range(PIPES), range(SIDE), range(SIDE))
]
PLANES_XY = [
    [p * FSDP + place(x, z, y) for x, y in itertools.product(range(SIDE), range(SIDE))]
    for p, z in itertools.product(range(PIPES), range(SIDE))
]


def hop(value, moves):
    pairs = [(a * FSDP + f, b * FSDP + f) for a, b in moves for f in range(FSDP)]
    return lax.ppermute(value, AXES, pairs)


def share(value, groups):
    count = len(groups[0])
    copies = jnp.broadcast_to(value[None], (count,) + value.shape)
    return lax.all_to_all(copies, AXES, 0, 0, axis_index_groups=groups)


def gather_channels(block):
    return share(share(block, LINES_Z), PLANES_XY)


def toeplitz_kernel(base_ref, out_ref):
    row = lax.broadcasted_iota(jnp.int32, (SEQ, TABLE), 0)
    column = lax.broadcasted_iota(jnp.int32, (SEQ, TABLE), 1)
    for index in range(base_ref.shape[0]):
        base = jnp.broadcast_to(base_ref[index : index + 1, :], (SEQ, TABLE))
        turned = pltpu.roll(base, 0, 1, stride=1, stride_axis=0)
        out_ref[index] = jnp.where(column <= row, turned, 0.0).astype(BF16)


def toeplitz(long_taps):
    count = long_taps.shape[0]
    base = jnp.concatenate(
        [long_taps[:, :1], jnp.zeros((count, TABLE - LANES), F32), long_taps[:, :0:-1]], axis=1
    )
    return pl.pallas_call(
        toeplitz_kernel,
        out_shape=jax.ShapeDtypeStruct((count, SEQ, TABLE), BF16),
        name="toeplitz",
    )(base)


def fetch(layer, weights_ref, held, sems):
    copies = []
    for x in range(SIDE):
        source, target = weights_ref.at[layer, ..., x, :, :, :, :], held.at[..., x, :, :, :, :]
        copies.append(pltpu.make_async_copy(source, target, sems.at[x]))
    for copy in copies:
        copy.start()
    return copies


def mix_kernel(layer, x_ref, gain_ref, w_ref, taps_ref, toep_ref, out_ref, held, sems, total, padded):
    copies = fetch(layer, w_ref, held, sems)
    power = jnp.zeros((SEQ, LANES), F32)
    for x in range(SIDE):
        scaled = []
        for z in range(SIDE):
            for y in range(SIDE):
                wide = x_ref[x * SIDE + y, z, :SEQ].astype(F32)
                power = power + wide * wide
                gain = gain_ref[x * SIDE + y, z].astype(F32)[layer : layer + 1, :]
                scaled.append((wide * gain).astype(BF16))
        left = jnp.concatenate(scaled, axis=1)
        copies[x].wait()
        right = jnp.concatenate(
            [held[j, x].reshape(SIDE * SIDE * LANES, LANES) for j in range(3)], axis=1
        )
        term = jnp.dot(left, right, preferred_element_type=F32)
        total[...] = term if x == 0 else total[...] + term

    mean = jnp.sum(power, axis=1, keepdims=True) / D
    inverse = lax.rsqrt(mean + 1e-06)
    mixed = []
    for j in range(3):
        projected = (total[:, j * LANES : (j + 1) * LANES] * inverse).astype(BF16)
        padded[j, :EXTRA] = jnp.zeros((EXTRA, LANES), F32)
        padded[j, EXTRA:] = projected.astype(F32)
        running = jnp.zeros((SEQ, LANES), F32)
        for i in range(STAPS):
            tap = taps_ref[j * STAPS + i : j * STAPS + i + 1, :]
            running = running + tap * padded[j, EXTRA - i : EXTRA - i + SEQ, :]
        mixed.append(running)
    product = mixed[1] * mixed[2]
    carried = taps_ref[3 * STAPS : 3 * STAPS + 1, :] * product
    lane = lax.broadcasted_iota(jnp.int32, (TABLE, LANES), 1)
    tall = jnp.concatenate([product, jnp.zeros((TABLE - SEQ, LANES), F32)], axis=0)
    for f in range(LANES // GROUP):
        kept = jnp.where(lane // GROUP == f, tall, 0.0).astype(BF16)
        carried = carried + jnp.dot(toep_ref[layer, f], kept, preferred_element_type=F32)
    out_ref[...] = (mixed[0] * carried).astype(BF16)


VMEM = pl.BlockSpec(memory_space=pltpu.VMEM)
HBM = pl.BlockSpec(memory_space=pltpu.HBM)


def mix(layer, gathered, gains, weights, taps, toep):
    def kernel(*refs):
        mix_kernel(layer, *refs)

    return pl.pallas_call(
        kernel,
        in_specs=[VMEM, VMEM, HBM, VMEM, VMEM],
        out_specs=VMEM,
        out_shape=jax.ShapeDtypeStruct((SEQ, LANES), BF16),
        scratch_shapes=[
            pltpu.VMEM((3, SIDE, SIDE, SIDE, LANES, LANES), BF16),
            pltpu.SemaphoreType.DMA((SIDE,)),
            pltpu.VMEM((SEQ, 3 * LANES), F32),
            pltpu.VMEM((3, EXTRA + SEQ, LANES), F32),
        ],
        compiler_params=pltpu.CompilerParams(vmem_limit_bytes=VMEM_LIMIT),
        name="mix",
    )(gathered, gains, weights, taps, toep)


def out_kernel(layer, g_ref, w_ref, x_ref, out_ref, held, sems, total):
    copies = fetch(layer, w_ref, held, sems)
    total[...] = x_ref[...].astype(F32)
    for x in range(SIDE):
        left = jnp.concatenate(
            [g_ref[x * SIDE + y, z] for z in range(SIDE) for y in range(SIDE)], axis=1
        )
        copies[x].wait()
        right = held[x].reshape(SIDE * SIDE * LANES, LANES)
        total[...] += jnp.dot(left, right, preferred_element_type=F32)
    out_ref[...] = total[...].astype(BF16)


def project_out(layer, gathered, weights, activation):
    def kernel(*refs):
        out_kernel(layer, *refs)

    return pl.pallas_call(
        kernel,
        in_specs=[VMEM, HBM, VMEM],
        out_specs=VMEM,
        out_shape=jax.ShapeDtypeStruct((SEQ, LANES), BF16),
        scratch_shapes=[
            pltpu.VMEM((SIDE, SIDE, SIDE, LANES, LANES), BF16),
            pltpu.SemaphoreType.DMA((SIDE,)),
            pltpu.VMEM((SEQ, LANES), F32),
        ],
        compiler_params=pltpu.CompilerParams(vmem_limit_bytes=VMEM_LIMIT),
        name="project_out",
    )(gathered, weights, activation)


CORES = [[0, 1], [2, 3]]


def body(tokens, embed, gain, w_in, short_filter, long_filter, skip_bias, w_out):
    core = lax.axis_index("pipe") % 2
    swap = [(0, 1), (1, 0), (2, 3), (3, 2)]

    own = jnp.concatenate(
        [
            short_filter[0].reshape(3 * STAPS, LANES),
            skip_bias,
            gain.astype(F32),
            jnp.zeros((1, LANES), F32),
            long_filter[0],
        ],
        axis=0,
    )
    other = hop(own, swap)
    first, second = jnp.where(core == 0, own, other), jnp.where(core == 0, other, own)
    w_in_both = lax.all_gather(w_in[0], "pipe", axis_index_groups=CORES)
    w_out_both = lax.all_gather(w_out[0], "pipe", axis_index_groups=CORES)
    w_in_both = w_in_both.reshape(2, 3, SIDE, SIDE, SIDE, LANES, LANES)
    w_out_both = w_out_both.reshape(2, SIDE, SIDE, SIDE, LANES, LANES)
    rows = 3 * STAPS + 3
    taps = [first[:rows], second[:rows]]
    toep = toeplitz(jnp.concatenate([first[rows:], second[rows:]], axis=0))
    toep = toep.reshape(2, LANES // GROUP, SEQ, TABLE)

    ids = lax.dynamic_index_in_dim(tokens, core, 0, keepdims=False)
    one_hot = (ids[:, None] == jnp.arange(embed.shape[0], dtype=jnp.int32)[None, :]).astype(BF16)
    activation = jnp.dot(one_hot, embed, preferred_element_type=F32).astype(BF16)

    gain_rows = jnp.concatenate(
        [first[rows - 2 : rows - 1], second[rows - 2 : rows - 1], jnp.zeros((EXTRA - 2, LANES), F32)],
        axis=0,
    )
    arrived = gather_channels(jnp.concatenate([activation, gain_rows.astype(BF16)], axis=0))
    gathered, gains = arrived, arrived[:, :, SEQ:]
    for part in range(2):
        for layer in range(2):
            if part + layer > 0:
                gathered = gather_channels(activation)
            gated = mix(layer, gathered, gains, w_in_both, taps[layer], toep)
            activation = project_out(layer, gather_channels(gated), w_out_both, activation)
        if part == 0:
            activation = hop(activation, [(0, 2), (1, 3)])

    quarters = activation.reshape(4, SEQ // 4, LANES)
    even, odd = quarters[0::2], quarters[1::2]
    keep = jnp.where(core == 0, even, odd)
    taken = hop(jnp.where(core == 0, odd, even), swap)
    row_0, row_1 = jnp.where(core == 0, keep, taken), jnp.where(core == 0, taken, keep)
    low, high = jnp.stack([row_0[0], row_1[0]]), jnp.stack([row_0[1], row_1[1]])
    passed = hop(low, [(2, 0), (3, 1)])
    return jnp.where(lax.axis_index("pipe") < 2, passed, high)


def solution(mesh):
    return jax.shard_map(
        body,
        mesh=mesh,
        in_specs=(
            P(),
            P(None, "fsdp"),
            P("pipe", "fsdp"),
            P("pipe", None, None, "fsdp"),
            P("pipe", None, None, "fsdp"),
            P("pipe", "fsdp", None),
            P("pipe", "fsdp"),
            P("pipe", None, "fsdp"),
        ),
        out_specs=P(None, "pipe", "fsdp"),
        check_vma=False,
    )
```

```python
import itertools

import jax
import jax.numpy as jnp
from jax import lax
from jax.experimental import pallas as pl
from jax.experimental.pallas import tpu as pltpu
from jax.sharding import PartitionSpec as P

D = 8192
STAPS = 7
SEQ = 160
LANES = 128
GROUP = 16
TABLE = 256
SIDE = 4
AXES = ("pipe", "fsdp")
PIPES = 4
FSDP = 64
EXTRA = 16
VMEM_LIMIT = 48 << 20
F32 = jnp.float32
BF16 = jnp.bfloat16


def place(x, z, y):
    return (x * SIDE + z) * SIDE + y


LINES_Z = [
    [p * FSDP + place(x, z, y) for z in range(SIDE)]
    for p, x, y in itertools.product(range(PIPES), range(SIDE), range(SIDE))
]
PLANES_XY = [
    [p * FSDP + place(x, z, y) for x, y in itertools.product(range(SIDE), range(SIDE))]
    for p, z in itertools.product(range(PIPES), range(SIDE))
]


def hop(value, moves):
    pairs = [(a * FSDP + f, b * FSDP + f) for a, b in moves for f in range(FSDP)]
    return lax.ppermute(value, AXES, pairs)


def share(value, groups):
    count = len(groups[0])
    copies = jnp.broadcast_to(value[None], (count,) + value.shape)
    return lax.all_to_all(copies, AXES, 0, 0, axis_index_groups=groups)


def gather_channels(block):
    return share(share(block, LINES_Z), PLANES_XY)


def gather_in_turn(block, core):
    copies = jnp.broadcast_to(block[None], (SIDE,) + block.shape)
    ahead = lax.cond(core == 1, lambda b: share(b, LINES_Z), lambda b: copies, block)
    turn = hop(ahead[0, :EXTRA], [(1, 0), (3, 2)])
    block = jnp.concatenate([block[: SEQ + 2], turn[2:]], axis=0)
    line = lax.cond(core == 0, lambda b, a: share(b, LINES_Z), lambda b, a: a, block, ahead)
    return share(line, PLANES_XY)


def toeplitz_kernel(base_ref, out_ref):
    row = lax.broadcasted_iota(jnp.int32, (SEQ, TABLE), 0)
    column = lax.broadcasted_iota(jnp.int32, (SEQ, TABLE), 1)
    for index in range(base_ref.shape[0]):
        base = jnp.broadcast_to(base_ref[index : index + 1, :], (SEQ, TABLE))
        turned = pltpu.roll(base, 0, 1, stride=1, stride_axis=0)
        out_ref[index] = jnp.where(column <= row, turned, 0.0).astype(BF16)


def toeplitz(long_taps):
    count = long_taps.shape[0]
    base = jnp.concatenate(
        [long_taps[:, :1], jnp.zeros((count, TABLE - LANES), F32), long_taps[:, :0:-1]], axis=1
    )
    return pl.pallas_call(
        toeplitz_kernel,
        out_shape=jax.ShapeDtypeStruct((count, SEQ, TABLE), BF16),
        name="toeplitz",
    )(base)


def fetch(layer, weights_ref, held, sems):
    copies = []
    for x in range(SIDE):
        source, target = weights_ref.at[layer, ..., x, :, :, :, :], held.at[..., x, :, :, :, :]
        copies.append(pltpu.make_async_copy(source, target, sems.at[x]))
    for copy in copies:
        copy.start()
    return copies


def mix_kernel(layer, x_ref, gain_ref, w_ref, taps_ref, toep_ref, out_ref, held, sems, total, padded):
    copies = fetch(layer, w_ref, held, sems)
    power = jnp.zeros((SEQ, LANES), F32)
    for x in range(SIDE):
        scaled = []
        for z in range(SIDE):
            for y in range(SIDE):
                wide = x_ref[x * SIDE + y, z, :SEQ].astype(F32)
                power = power + wide * wide
                gain = gain_ref[x * SIDE + y, z].astype(F32)[layer : layer + 1, :]
                scaled.append((wide * gain).astype(BF16))
        left = jnp.concatenate(scaled, axis=1)
        copies[x].wait()
        right = jnp.concatenate(
            [held[j, x].reshape(SIDE * SIDE * LANES, LANES) for j in range(3)], axis=1
        )
        term = jnp.dot(left, right, preferred_element_type=F32)
        total[...] = term if x == 0 else total[...] + term

    mean = jnp.sum(power, axis=1, keepdims=True) / D
    inverse = lax.rsqrt(mean + 1e-06)
    mixed = []
    for j in range(3):
        projected = (total[:, j * LANES : (j + 1) * LANES] * inverse).astype(BF16)
        padded[j, :EXTRA] = jnp.zeros((EXTRA, LANES), F32)
        padded[j, EXTRA:] = projected.astype(F32)
        running = jnp.zeros((SEQ, LANES), F32)
        for i in range(STAPS):
            tap = taps_ref[j * STAPS + i : j * STAPS + i + 1, :]
            running = running + tap * padded[j, EXTRA - i : EXTRA - i + SEQ, :]
        mixed.append(running)
    product = mixed[1] * mixed[2]
    carried = taps_ref[3 * STAPS : 3 * STAPS + 1, :] * product
    lane = lax.broadcasted_iota(jnp.int32, (TABLE, LANES), 1)
    tall = jnp.concatenate([product, jnp.zeros((TABLE - SEQ, LANES), F32)], axis=0)
    for f in range(LANES // GROUP):
        kept = jnp.where(lane // GROUP == f, tall, 0.0).astype(BF16)
        carried = carried + jnp.dot(toep_ref[layer, f], kept, preferred_element_type=F32)
    out_ref[...] = (mixed[0] * carried).astype(BF16)


VMEM = pl.BlockSpec(memory_space=pltpu.VMEM)
HBM = pl.BlockSpec(memory_space=pltpu.HBM)


def mix(layer, gathered, gains, weights, taps, toep):
    def kernel(*refs):
        mix_kernel(layer, *refs)

    return pl.pallas_call(
        kernel,
        in_specs=[VMEM, VMEM, HBM, VMEM, VMEM],
        out_specs=VMEM,
        out_shape=jax.ShapeDtypeStruct((SEQ, LANES), BF16),
        scratch_shapes=[
            pltpu.VMEM((3, SIDE, SIDE, SIDE, LANES, LANES), BF16),
            pltpu.SemaphoreType.DMA((SIDE,)),
            pltpu.VMEM((SEQ, 3 * LANES), F32),
            pltpu.VMEM((3, EXTRA + SEQ, LANES), F32),
        ],
        compiler_params=pltpu.CompilerParams(vmem_limit_bytes=VMEM_LIMIT),
        name="mix",
    )(gathered, gains, weights, taps, toep)


def out_kernel(layer, g_ref, w_ref, x_ref, out_ref, held, sems, total):
    copies = fetch(layer, w_ref, held, sems)
    total[...] = x_ref[...].astype(F32)
    for x in range(SIDE):
        left = jnp.concatenate(
            [g_ref[x * SIDE + y, z] for z in range(SIDE) for y in range(SIDE)], axis=1
        )
        copies[x].wait()
        right = held[x].reshape(SIDE * SIDE * LANES, LANES)
        total[...] += jnp.dot(left, right, preferred_element_type=F32)
    out_ref[...] = total[...].astype(BF16)


def project_out(layer, gathered, weights, activation):
    def kernel(*refs):
        out_kernel(layer, *refs)

    return pl.pallas_call(
        kernel,
        in_specs=[VMEM, HBM, VMEM],
        out_specs=VMEM,
        out_shape=jax.ShapeDtypeStruct((SEQ, LANES), BF16),
        scratch_shapes=[
            pltpu.VMEM((SIDE, SIDE, SIDE, LANES, LANES), BF16),
            pltpu.SemaphoreType.DMA((SIDE,)),
            pltpu.VMEM((SEQ, LANES), F32),
        ],
        compiler_params=pltpu.CompilerParams(vmem_limit_bytes=VMEM_LIMIT),
        name="project_out",
    )(gathered, weights, activation)


CORES = [[0, 1], [2, 3]]


def body(tokens, embed, gain, w_in, short_filter, long_filter, skip_bias, w_out):
    core = lax.axis_index("pipe") % 2
    swap = [(0, 1), (1, 0), (2, 3), (3, 2)]

    own = jnp.concatenate(
        [
            short_filter[0].reshape(3 * STAPS, LANES),
            skip_bias,
            gain.astype(F32),
            jnp.zeros((1, LANES), F32),
            long_filter[0],
        ],
        axis=0,
    )
    other = hop(own, swap)
    first, second = jnp.where(core == 0, own, other), jnp.where(core == 0, other, own)
    w_in_both = lax.all_gather(w_in[0], "pipe", axis_index_groups=CORES)
    w_out_both = lax.all_gather(w_out[0], "pipe", axis_index_groups=CORES)
    w_in_both = w_in_both.reshape(2, 3, SIDE, SIDE, SIDE, LANES, LANES)
    w_out_both = w_out_both.reshape(2, SIDE, SIDE, SIDE, LANES, LANES)
    rows = 3 * STAPS + 3
    taps = [first[:rows], second[:rows]]
    toep = toeplitz(jnp.concatenate([first[rows:], second[rows:]], axis=0))
    toep = toep.reshape(2, LANES // GROUP, SEQ, TABLE)

    ids = lax.dynamic_index_in_dim(tokens, core, 0, keepdims=False)
    one_hot = (ids[:, None] == jnp.arange(embed.shape[0], dtype=jnp.int32)[None, :]).astype(BF16)
    activation = jnp.dot(one_hot, embed, preferred_element_type=F32).astype(BF16)

    gain_rows = jnp.concatenate(
        [first[rows - 2 : rows - 1], second[rows - 2 : rows - 1], jnp.zeros((EXTRA - 2, LANES), F32)],
        axis=0,
    )
    arrived = gather_in_turn(
        jnp.concatenate([activation, gain_rows.astype(BF16)], axis=0), core
    )
    gathered, gains = arrived, arrived[:, :, SEQ:]
    for part in range(2):
        for layer in range(2):
            if part + layer > 0:
                gathered = gather_channels(activation)
            gated = mix(layer, gathered, gains, w_in_both, taps[layer], toep)
            activation = project_out(layer, gather_channels(gated), w_out_both, activation)
        if part == 0:
            activation = hop(activation, [(0, 2), (1, 3)])

    quarters = activation.reshape(4, SEQ // 4, LANES)
    even, odd = quarters[0::2], quarters[1::2]
    keep = jnp.where(core == 0, even, odd)
    taken = hop(jnp.where(core == 0, odd, even), swap)
    row_0, row_1 = jnp.where(core == 0, keep, taken), jnp.where(core == 0, taken, keep)
    low, high = jnp.stack([row_0[0], row_1[0]]), jnp.stack([row_0[1], row_1[1]])
    passed = hop(low, [(2, 0), (3, 1)])
    return jnp.where(lax.axis_index("pipe") < 2, passed, high)


def solution(mesh):
    return jax.shard_map(
        body,
        mesh=mesh,
        in_specs=(
            P(),
            P(None, "fsdp"),
            P("pipe", "fsdp"),
            P("pipe", None, None, "fsdp"),
            P("pipe", None, None, "fsdp"),
            P("pipe", "fsdp", None),
            P("pipe", "fsdp"),
            P("pipe", None, "fsdp"),
        ),
        out_specs=P(None, "pipe", "fsdp"),
        check_vma=False,
    )
```

```python
import itertools

import jax
import jax.numpy as jnp
from jax import lax
from jax.experimental import pallas as pl
from jax.experimental.pallas import tpu as pltpu
from jax.sharding import PartitionSpec as P

D = 8192
STAPS = 7
SEQ = 160
LANES = 128
GROUP = 16
TABLE = 256
SIDE = 4
AXES = ("pipe", "fsdp")
PIPES = 4
FSDP = 64
EXTRA = 16
VMEM_LIMIT = 48 << 20
F32 = jnp.float32
BF16 = jnp.bfloat16


def place(x, z, y):
    return (x * SIDE + z) * SIDE + y


LINES_Z = [
    [p * FSDP + place(x, z, y) for z in range(SIDE)]
    for p, x, y in itertools.product(range(PIPES), range(SIDE), range(SIDE))
]
PLANES_XY = [
    [p * FSDP + place(x, z, y) for x, y in itertools.product(range(SIDE), range(SIDE))]
    for p, z in itertools.product(range(PIPES), range(SIDE))
]


def hop(value, moves):
    pairs = [(a * FSDP + f, b * FSDP + f) for a, b in moves for f in range(FSDP)]
    return lax.ppermute(value, AXES, pairs)


def share(value, groups):
    count = len(groups[0])
    copies = jnp.broadcast_to(value[None], (count,) + value.shape)
    return lax.all_to_all(copies, AXES, 0, 0, axis_index_groups=groups)


def gather_channels(block):
    return share(share(block, LINES_Z), PLANES_XY)


def toeplitz_kernel(base_ref, out_ref):
    row = lax.broadcasted_iota(jnp.int32, (SEQ, TABLE), 0)
    column = lax.broadcasted_iota(jnp.int32, (SEQ, TABLE), 1)
    for index in range(base_ref.shape[0]):
        base = jnp.broadcast_to(base_ref[index : index + 1, :], (SEQ, TABLE))
        turned = pltpu.roll(base, 0, 1, stride=1, stride_axis=0)
        out_ref[index] = jnp.where(column <= row, turned, 0.0).astype(BF16)


def toeplitz(long_taps):
    count = long_taps.shape[0]
    base = jnp.concatenate(
        [long_taps[:, :1], jnp.zeros((count, TABLE - LANES), F32), long_taps[:, :0:-1]], axis=1
    )
    return pl.pallas_call(
        toeplitz_kernel,
        out_shape=jax.ShapeDtypeStruct((count, SEQ, TABLE), BF16),
        name="toeplitz",
    )(base)


def fetch(layer, core_ref, own_ref, other_ref, held, sems):
    def copies(source):
        return [
            pltpu.make_async_copy(
                source.at[..., x, :, :, :, :], held.at[..., x, :, :, :, :], sems.at[x]
            )
            for x in range(SIDE)
        ]

    @pl.when(core_ref[0] == layer)
    def _():
        for copy in copies(own_ref):
            copy.start()

    @pl.when(core_ref[0] != layer)
    def _():
        for copy in copies(other_ref):
            copy.start()

    return copies(own_ref)


def mix_kernel(
    layer, core_ref, x_ref, gain_ref, own_ref, other_ref, taps_ref, toep_ref, out_ref,
    held, sems, total, padded,
):
    copies = fetch(layer, core_ref, own_ref, other_ref, held, sems)
    power = jnp.zeros((SEQ, LANES), F32)
    for x in range(SIDE):
        scaled = []
        for z in range(SIDE):
            for y in range(SIDE):
                wide = x_ref[x * SIDE + y, z, :SEQ].astype(F32)
                power = power + wide * wide
                gain = gain_ref[x * SIDE + y, z].astype(F32)[layer : layer + 1, :]
                scaled.append((wide * gain).astype(BF16))
        left = jnp.concatenate(scaled, axis=1)
        copies[x].wait()
        right = jnp.concatenate(
            [held[j, x].reshape(SIDE * SIDE * LANES, LANES) for j in range(3)], axis=1
        )
        term = jnp.dot(left, right, preferred_element_type=F32)
        total[...] = term if x == 0 else total[...] + term

    mean = jnp.sum(power, axis=1, keepdims=True) / D
    inverse = lax.rsqrt(mean + 1e-06)
    mixed = []
    for j in range(3):
        projected = (total[:, j * LANES : (j + 1) * LANES] * inverse).astype(BF16)
        padded[j, :EXTRA] = jnp.zeros((EXTRA, LANES), F32)
        padded[j, EXTRA:] = projected.astype(F32)
        running = jnp.zeros((SEQ, LANES), F32)
        for i in range(STAPS):
            tap = taps_ref[j * STAPS + i : j * STAPS + i + 1, :]
            running = running + tap * padded[j, EXTRA - i : EXTRA - i + SEQ, :]
        mixed.append(running)
    product = mixed[1] * mixed[2]
    carried = taps_ref[3 * STAPS : 3 * STAPS + 1, :] * product
    lane = lax.broadcasted_iota(jnp.int32, (TABLE, LANES), 1)
    tall = jnp.concatenate([product, jnp.zeros((TABLE - SEQ, LANES), F32)], axis=0)
    for f in range(LANES // GROUP):
        kept = jnp.where(lane // GROUP == f, tall, 0.0).astype(BF16)
        carried = carried + jnp.dot(toep_ref[layer, f], kept, preferred_element_type=F32)
    out_ref[...] = (mixed[0] * carried).astype(BF16)


SMEM = pl.BlockSpec(memory_space=pltpu.SMEM)
VMEM = pl.BlockSpec(memory_space=pltpu.VMEM)
HBM = pl.BlockSpec(memory_space=pltpu.HBM)


def mix(layer, core, gathered, gains, weights, taps, toep):
    def kernel(*refs):
        mix_kernel(layer, *refs)

    return pl.pallas_call(
        kernel,
        in_specs=[SMEM, VMEM, VMEM, HBM, HBM, VMEM, VMEM],
        out_specs=VMEM,
        out_shape=jax.ShapeDtypeStruct((SEQ, LANES), BF16),
        scratch_shapes=[
            pltpu.VMEM((3, SIDE, SIDE, SIDE, LANES, LANES), BF16),
            pltpu.SemaphoreType.DMA((SIDE,)),
            pltpu.VMEM((SEQ, 3 * LANES), F32),
            pltpu.VMEM((3, EXTRA + SEQ, LANES), F32),
        ],
        compiler_params=pltpu.CompilerParams(vmem_limit_bytes=VMEM_LIMIT),
        name="mix",
    )(core, gathered, gains, *weights, taps, toep)


def out_kernel(
    layer, core_ref, g_ref, own_ref, other_ref, x_ref, out_ref, held, sems, total
):
    copies = fetch(layer, core_ref, own_ref, other_ref, held, sems)
    total[...] = x_ref[...].astype(F32)
    for x in range(SIDE):
        left = jnp.concatenate(
            [g_ref[x * SIDE + y, z] for z in range(SIDE) for y in range(SIDE)], axis=1
        )
        copies[x].wait()
        right = held[x].reshape(SIDE * SIDE * LANES, LANES)
        total[...] += jnp.dot(left, right, preferred_element_type=F32)
    out_ref[...] = total[...].astype(BF16)


def project_out(layer, core, gathered, weights, activation):
    def kernel(*refs):
        out_kernel(layer, *refs)

    return pl.pallas_call(
        kernel,
        in_specs=[SMEM, VMEM, HBM, HBM, VMEM],
        out_specs=VMEM,
        out_shape=jax.ShapeDtypeStruct((SEQ, LANES), BF16),
        scratch_shapes=[
            pltpu.VMEM((SIDE, SIDE, SIDE, LANES, LANES), BF16),
            pltpu.SemaphoreType.DMA((SIDE,)),
            pltpu.VMEM((SEQ, LANES), F32),
        ],
        compiler_params=pltpu.CompilerParams(vmem_limit_bytes=VMEM_LIMIT),
        name="project_out",
    )(core, gathered, *weights, activation)


def body(tokens, embed, gain, w_in, short_filter, long_filter, skip_bias, w_out):
    core = lax.axis_index("pipe") % 2
    place_in_chip = jnp.reshape(core, (1,)).astype(jnp.int32)
    swap = [(0, 1), (1, 0), (2, 3), (3, 2)]

    own = jnp.concatenate(
        [
            short_filter[0].reshape(3 * STAPS, LANES),
            skip_bias,
            gain.astype(F32),
            jnp.zeros((1, LANES), F32),
            long_filter[0],
        ],
        axis=0,
    )
    other = hop(own, swap)
    first, second = jnp.where(core == 0, own, other), jnp.where(core == 0, other, own)
    w_in_own = w_in.reshape(3, SIDE, SIDE, SIDE, LANES, LANES)
    w_out_own = w_out.reshape(SIDE, SIDE, SIDE, LANES, LANES)
    rows = 3 * STAPS + 3
    taps = [first[:rows], second[:rows]]
    toep = toeplitz(jnp.concatenate([first[rows:], second[rows:]], axis=0))
    toep = toep.reshape(2, LANES // GROUP, SEQ, TABLE)

    ids = lax.dynamic_index_in_dim(tokens, core, 0, keepdims=False)
    one_hot = (ids[:, None] == jnp.arange(embed.shape[0], dtype=jnp.int32)[None, :]).astype(BF16)
    activation = jnp.dot(one_hot, embed, preferred_element_type=F32).astype(BF16)

    gain_rows = jnp.concatenate(
        [first[rows - 2 : rows - 1], second[rows - 2 : rows - 1], jnp.zeros((EXTRA - 2, LANES), F32)],
        axis=0,
    )
    def layers(activation, w_in_other, w_out_other):
        arrived = gather_channels(jnp.concatenate([activation, gain_rows.astype(BF16)], axis=0))
        gathered, gains = arrived, arrived[:, :, SEQ:]
        for layer in range(2):
            if layer > 0:
                gathered = gather_channels(activation)
            gated = mix(
                layer, place_in_chip, gathered, gains, (w_in_own, w_in_other), taps[layer], toep
            )
            activation = project_out(
                layer, place_in_chip, gather_channels(gated), (w_out_own, w_out_other), activation
            )
        return activation

    def first_chips(activation):
        others = hop(w_in_own, swap[:2]), hop(w_out_own, swap[:2])
        return layers(activation, *others), *others

    def later_chips(activation):
        return activation, hop(w_in_own, swap[2:]), hop(w_out_own, swap[2:])

    leading = lax.axis_index("pipe") < 2
    activation, *others = lax.cond(leading, first_chips, later_chips, activation)
    activation = hop(activation, [(0, 2), (1, 3)])
    activation = lax.cond(leading, lambda a, *_: a, layers, activation, *others)

    quarters = activation.reshape(4, SEQ // 4, LANES)
    even, odd = quarters[0::2], quarters[1::2]
    keep = jnp.where(core == 0, even, odd)
    taken = hop(jnp.where(core == 0, odd, even), swap)
    row_0, row_1 = jnp.where(core == 0, keep, taken), jnp.where(core == 0, taken, keep)
    low, high = jnp.stack([row_0[0], row_1[0]]), jnp.stack([row_0[1], row_1[1]])
    passed = hop(low, [(2, 0), (3, 1)])
    return jnp.where(lax.axis_index("pipe") < 2, passed, high)


def solution(mesh):
    return jax.shard_map(
        body,
        mesh=mesh,
        in_specs=(
            P(),
            P(None, "fsdp"),
            P("pipe", "fsdp"),
            P("pipe", None, None, "fsdp"),
            P("pipe", None, None, "fsdp"),
            P("pipe", "fsdp", None),
            P("pipe", "fsdp"),
            P("pipe", None, "fsdp"),
        ),
        out_specs=P(None, "pipe", "fsdp"),
        check_vma=False,
    )
```

```python
import itertools

import jax
import jax.numpy as jnp
from jax import lax
from jax.experimental import pallas as pl
from jax.experimental.pallas import tpu as pltpu
from jax.sharding import PartitionSpec as P

D = 8192
STAPS = 7
SEQ = 160
LANES = 128
GROUP = 16
TABLE = 256
SIDE = 4
AXES = ("pipe", "fsdp")
PIPES = 4
FSDP = 64
EXTRA = 16
VMEM_LIMIT = 48 << 20
F32 = jnp.float32
BF16 = jnp.bfloat16


def place(x, z, y):
    return (x * SIDE + z) * SIDE + y


LINES_Z = [
    [p * FSDP + place(x, z, y) for z in range(SIDE)]
    for p, x, y in itertools.product(range(PIPES), range(SIDE), range(SIDE))
]
PLANES_XY = [
    [p * FSDP + place(x, z, y) for x, y in itertools.product(range(SIDE), range(SIDE))]
    for p, z in itertools.product(range(PIPES), range(SIDE))
]


def hop(value, moves):
    pairs = [(a * FSDP + f, b * FSDP + f) for a, b in moves for f in range(FSDP)]
    return lax.ppermute(value, AXES, pairs)


def share(value, groups):
    count = len(groups[0])
    copies = jnp.broadcast_to(value[None], (count,) + value.shape)
    return lax.all_to_all(copies, AXES, 0, 0, axis_index_groups=groups)


def gather_channels(block):
    return share(share(block, LINES_Z), PLANES_XY)


def toeplitz_kernel(base_ref, out_ref):
    row = lax.broadcasted_iota(jnp.int32, (SEQ, TABLE), 0)
    column = lax.broadcasted_iota(jnp.int32, (SEQ, TABLE), 1)
    for index in range(base_ref.shape[0]):
        base = jnp.broadcast_to(base_ref[index : index + 1, :], (SEQ, TABLE))
        turned = pltpu.roll(base, 0, 1, stride=1, stride_axis=0)
        out_ref[index] = jnp.where(column <= row, turned, 0.0).astype(BF16)


def toeplitz(long_taps):
    count = long_taps.shape[0]
    base = jnp.concatenate(
        [long_taps[:, :1], jnp.zeros((count, TABLE - LANES), F32), long_taps[:, :0:-1]], axis=1
    )
    return pl.pallas_call(
        toeplitz_kernel,
        out_shape=jax.ShapeDtypeStruct((count, SEQ, TABLE), BF16),
        name="toeplitz",
    )(base)


def fetch(layer, core_ref, own_ref, other_ref, held, sems):
    def copies(source):
        return [
            pltpu.make_async_copy(
                source.at[..., x, :, :, :, :], held.at[..., x, :, :, :, :], sems.at[x]
            )
            for x in range(SIDE)
        ]

    @pl.when(core_ref[0] == layer)
    def _():
        for copy in copies(own_ref):
            copy.start()

    @pl.when(core_ref[0] != layer)
    def _():
        for copy in copies(other_ref):
            copy.start()

    return copies(own_ref)


def mix_kernel(
    layer, core_ref, x_ref, gain_ref, own_ref, other_ref, taps_ref, toep_ref, out_ref,
    held, sems, total, padded,
):
    copies = fetch(layer, core_ref, own_ref, other_ref, held, sems)
    power = jnp.zeros((SEQ, LANES), F32)
    for x in range(SIDE):
        scaled = []
        for z in range(SIDE):
            for y in range(SIDE):
                wide = x_ref[x * SIDE + y, z, :SEQ].astype(F32)
                power = power + wide * wide
                gain = gain_ref[x * SIDE + y, z].astype(F32)[layer : layer + 1, :]
                scaled.append((wide * gain).astype(BF16))
        left = jnp.concatenate(scaled, axis=1)
        copies[x].wait()
        right = jnp.concatenate(
            [held[j, x].reshape(SIDE * SIDE * LANES, LANES) for j in range(3)], axis=1
        )
        term = jnp.dot(left, right, preferred_element_type=F32)
        total[...] = term if x == 0 else total[...] + term

    mean = jnp.sum(power, axis=1, keepdims=True) / D
    inverse = lax.rsqrt(mean + 1e-06)
    mixed = []
    for j in range(3):
        projected = (total[:, j * LANES : (j + 1) * LANES] * inverse).astype(BF16)
        padded[j, :EXTRA] = jnp.zeros((EXTRA, LANES), F32)
        padded[j, EXTRA:] = projected.astype(F32)
        running = jnp.zeros((SEQ, LANES), F32)
        for i in range(STAPS):
            tap = taps_ref[j * STAPS + i : j * STAPS + i + 1, :]
            running = running + tap * padded[j, EXTRA - i : EXTRA - i + SEQ, :]
        mixed.append(running)
    product = mixed[1] * mixed[2]
    carried = taps_ref[3 * STAPS : 3 * STAPS + 1, :] * product
    lane = lax.broadcasted_iota(jnp.int32, (TABLE, LANES), 1)
    tall = jnp.concatenate([product, jnp.zeros((TABLE - SEQ, LANES), F32)], axis=0)
    for f in range(LANES // GROUP):
        kept = jnp.where(lane // GROUP == f, tall, 0.0).astype(BF16)
        carried = carried + jnp.dot(toep_ref[layer, f], kept, preferred_element_type=F32)
    out_ref[...] = (mixed[0] * carried).astype(BF16)


SMEM = pl.BlockSpec(memory_space=pltpu.SMEM)
VMEM = pl.BlockSpec(memory_space=pltpu.VMEM)
HBM = pl.BlockSpec(memory_space=pltpu.HBM)


def mix(layer, core, gathered, gains, weights, taps, toep):
    def kernel(*refs):
        mix_kernel(layer, *refs)

    return pl.pallas_call(
        kernel,
        in_specs=[SMEM, VMEM, VMEM, HBM, HBM, VMEM, VMEM],
        out_specs=VMEM,
        out_shape=jax.ShapeDtypeStruct((SEQ, LANES), BF16),
        scratch_shapes=[
            pltpu.VMEM((3, SIDE, SIDE, SIDE, LANES, LANES), BF16),
            pltpu.SemaphoreType.DMA((SIDE,)),
            pltpu.VMEM((SEQ, 3 * LANES), F32),
            pltpu.VMEM((3, EXTRA + SEQ, LANES), F32),
        ],
        compiler_params=pltpu.CompilerParams(vmem_limit_bytes=VMEM_LIMIT),
        name="mix",
    )(core, gathered, gains, *weights, taps, toep)


def out_kernel(
    layer, core_ref, g_ref, own_ref, other_ref, x_ref, out_ref, held, sems, total
):
    copies = fetch(layer, core_ref, own_ref, other_ref, held, sems)
    total[...] = x_ref[...].astype(F32)
    for x in range(SIDE):
        left = jnp.concatenate(
            [g_ref[x * SIDE + y, z] for z in range(SIDE) for y in range(SIDE)], axis=1
        )
        copies[x].wait()
        right = held[x].reshape(SIDE * SIDE * LANES, LANES)
        total[...] += jnp.dot(left, right, preferred_element_type=F32)
    out_ref[...] = total[...].astype(BF16)


def project_out(layer, core, gathered, weights, activation):
    def kernel(*refs):
        out_kernel(layer, *refs)

    return pl.pallas_call(
        kernel,
        in_specs=[SMEM, VMEM, HBM, HBM, VMEM],
        out_specs=VMEM,
        out_shape=jax.ShapeDtypeStruct((SEQ, LANES), BF16),
        scratch_shapes=[
            pltpu.VMEM((SIDE, SIDE, SIDE, LANES, LANES), BF16),
            pltpu.SemaphoreType.DMA((SIDE,)),
            pltpu.VMEM((SEQ, LANES), F32),
        ],
        compiler_params=pltpu.CompilerParams(vmem_limit_bytes=VMEM_LIMIT),
        name="project_out",
    )(core, gathered, *weights, activation)


def body(tokens, embed, gain, w_in, short_filter, long_filter, skip_bias, w_out):
    core = lax.axis_index("pipe") % 2
    place_in_chip = jnp.reshape(core, (1,)).astype(jnp.int32)
    swap = [(0, 1), (1, 0), (2, 3), (3, 2)]

    own = jnp.concatenate(
        [
            short_filter[0].reshape(3 * STAPS, LANES),
            skip_bias,
            gain.astype(F32),
            jnp.zeros((1, LANES), F32),
            long_filter[0],
        ],
        axis=0,
    )
    other = hop(own, swap)
    first, second = jnp.where(core == 0, own, other), jnp.where(core == 0, other, own)
    w_in_own = w_in.reshape(3, SIDE, SIDE, SIDE, LANES, LANES)
    w_out_own = w_out.reshape(SIDE, SIDE, SIDE, LANES, LANES)
    rows = 3 * STAPS + 3
    taps = [first[:rows], second[:rows]]
    toep = toeplitz(jnp.concatenate([first[rows:], second[rows:]], axis=0))
    toep = toep.reshape(2, LANES // GROUP, SEQ, TABLE)

    ids = lax.dynamic_index_in_dim(tokens, core, 0, keepdims=False)
    one_hot = (ids[:, None] == jnp.arange(embed.shape[0], dtype=jnp.int32)[None, :]).astype(BF16)
    activation = jnp.dot(one_hot, embed, preferred_element_type=F32).astype(BF16)

    gain_rows = jnp.concatenate(
        [first[rows - 2 : rows - 1], second[rows - 2 : rows - 1], jnp.zeros((EXTRA - 2, LANES), F32)],
        axis=0,
    )
    def with_gains(activation):
        return jnp.concatenate([activation, gain_rows.astype(BF16)], axis=0)

    def layers(arrived, activation, w_in_other, w_out_other):
        gathered, gains = arrived, arrived[:, :, SEQ:]
        for layer in range(2):
            if layer > 0:
                gathered = gather_channels(activation)
            gated = mix(
                layer, place_in_chip, gathered, gains, (w_in_own, w_in_other), taps[layer], toep
            )
            activation = project_out(
                layer, place_in_chip, gather_channels(gated), (w_out_own, w_out_other), activation
            )
        return activation

    def first_chips(activation):
        block = with_gains(activation)
        others = hop(w_in_own, swap[:2]), hop(w_out_own, swap[:2])
        shape = (SIDE * SIDE, SIDE) + block.shape
        ahead = lax.cond(core == 1, gather_channels, lambda b: jnp.zeros(shape, BF16), block)
        block, ahead, *others = lax.optimization_barrier((block, ahead, *others))
        arrived = lax.cond(core == 0, lambda b, a: gather_channels(b), lambda b, a: a, block, ahead)
        return layers(arrived, activation, *others), *others

    def later_chips(activation):
        return activation, hop(w_in_own, swap[2:]), hop(w_out_own, swap[2:])

    leading = lax.axis_index("pipe") < 2
    activation, *others = lax.cond(leading, first_chips, later_chips, activation)
    activation = hop(activation, [(0, 2), (1, 3)])
    activation = lax.cond(
        leading,
        lambda a, *_: a,
        lambda a, *o: layers(gather_channels(with_gains(a)), a, *o),
        activation,
        *others,
    )

    quarters = activation.reshape(4, SEQ // 4, LANES)
    even, odd = quarters[0::2], quarters[1::2]
    keep = jnp.where(core == 0, even, odd)
    taken = hop(jnp.where(core == 0, odd, even), swap)
    row_0, row_1 = jnp.where(core == 0, keep, taken), jnp.where(core == 0, taken, keep)
    low, high = jnp.stack([row_0[0], row_1[0]]), jnp.stack([row_0[1], row_1[1]])
    passed = hop(low, [(2, 0), (3, 1)])
    return jnp.where(lax.axis_index("pipe") < 2, passed, high)


def solution(mesh):
    return jax.shard_map(
        body,
        mesh=mesh,
        in_specs=(
            P(),
            P(None, "fsdp"),
            P("pipe", "fsdp"),
            P("pipe", None, None, "fsdp"),
            P("pipe", None, None, "fsdp"),
            P("pipe", "fsdp", None),
            P("pipe", "fsdp"),
            P("pipe", None, "fsdp"),
        ),
        out_specs=P(None, "pipe", "fsdp"),
        check_vma=False,
    )
```

```python
import itertools

import jax
import jax.numpy as jnp
from jax import lax
from jax.experimental import pallas as pl
from jax.experimental.pallas import tpu as pltpu
from jax.sharding import PartitionSpec as P

D = 8192
STAPS = 7
SEQ = 160
LANES = 128
GROUP = 16
TABLE = 256
SIDE = 4
AXES = ("pipe", "fsdp")
PIPES = 4
FSDP = 64
EXTRA = 16
VMEM_LIMIT = 48 << 20
F32 = jnp.float32
BF16 = jnp.bfloat16


def place(x, z, y):
    return (x * SIDE + z) * SIDE + y


LINES_Z = [
    [p * FSDP + place(x, z, y) for z in range(SIDE)]
    for p, x, y in itertools.product(range(PIPES), range(SIDE), range(SIDE))
]
PLANES_XY = [
    [p * FSDP + place(x, z, y) for x, y in itertools.product(range(SIDE), range(SIDE))]
    for p, z in itertools.product(range(PIPES), range(SIDE))
]


def hop(value, moves):
    pairs = [(a * FSDP + f, b * FSDP + f) for a, b in moves for f in range(FSDP)]
    return lax.ppermute(value, AXES, pairs)


def share(value, groups):
    count = len(groups[0])
    copies = jnp.broadcast_to(value[None], (count,) + value.shape)
    return lax.all_to_all(copies, AXES, 0, 0, axis_index_groups=groups)


def gather_channels(block):
    return share(share(block, LINES_Z), PLANES_XY)


def toeplitz_kernel(base_ref, out_ref):
    row = lax.broadcasted_iota(jnp.int32, (SEQ, TABLE), 0)
    column = lax.broadcasted_iota(jnp.int32, (SEQ, TABLE), 1)
    for index in range(base_ref.shape[0]):
        base = jnp.broadcast_to(base_ref[index : index + 1, :], (SEQ, TABLE))
        turned = pltpu.roll(base, 0, 1, stride=1, stride_axis=0)
        out_ref[index] = jnp.where(column <= row, turned, 0.0).astype(BF16)


def toeplitz(long_taps):
    count = long_taps.shape[0]
    base = jnp.concatenate(
        [long_taps[:, :1], jnp.zeros((count, TABLE - LANES), F32), long_taps[:, :0:-1]], axis=1
    )
    return pl.pallas_call(
        toeplitz_kernel,
        out_shape=jax.ShapeDtypeStruct((count, SEQ, TABLE), BF16),
        name="toeplitz",
    )(base)


def fetch(layer, core_ref, own_ref, other_ref, held, sems):
    def copies(source):
        return [
            pltpu.make_async_copy(
                source.at[..., x, :, :, :, :], held.at[..., x, :, :, :, :], sems.at[x]
            )
            for x in range(SIDE)
        ]

    @pl.when(core_ref[0] == layer)
    def _():
        for copy in copies(own_ref):
            copy.start()

    @pl.when(core_ref[0] != layer)
    def _():
        for copy in copies(other_ref):
            copy.start()

    return copies(own_ref)


def mix_kernel(
    layer, core_ref, x_ref, gain_ref, own_ref, other_ref, taps_ref, toep_ref, out_ref,
    held, sems, total, padded,
):
    copies = fetch(layer, core_ref, own_ref, other_ref, held, sems)
    power = jnp.zeros((SEQ, LANES), F32)
    for x in range(SIDE):
        scaled = []
        for z in range(SIDE):
            for y in range(SIDE):
                wide = x_ref[x * SIDE + y, z, :SEQ].astype(F32)
                power = power + wide * wide
                gain = gain_ref[x * SIDE + y, z].astype(F32)[layer : layer + 1, :]
                scaled.append((wide * gain).astype(BF16))
        left = jnp.concatenate(scaled, axis=1)
        copies[x].wait()
        right = jnp.concatenate(
            [held[j, x].reshape(SIDE * SIDE * LANES, LANES) for j in range(3)], axis=1
        )
        term = jnp.dot(left, right, preferred_element_type=F32)
        total[...] = term if x == 0 else total[...] + term

    mean = jnp.sum(power, axis=1, keepdims=True) / D
    inverse = lax.rsqrt(mean + 1e-06)
    mixed = []
    for j in range(3):
        projected = (total[:, j * LANES : (j + 1) * LANES] * inverse).astype(BF16)
        padded[j, :EXTRA] = jnp.zeros((EXTRA, LANES), F32)
        padded[j, EXTRA:] = projected.astype(F32)
        running = jnp.zeros((SEQ, LANES), F32)
        for i in range(STAPS):
            tap = taps_ref[j * STAPS + i : j * STAPS + i + 1, :]
            running = running + tap * padded[j, EXTRA - i : EXTRA - i + SEQ, :]
        mixed.append(running)
    product = mixed[1] * mixed[2]
    carried = taps_ref[3 * STAPS : 3 * STAPS + 1, :] * product
    lane = lax.broadcasted_iota(jnp.int32, (TABLE, LANES), 1)
    tall = jnp.concatenate([product, jnp.zeros((TABLE - SEQ, LANES), F32)], axis=0)
    for f in range(LANES // GROUP):
        kept = jnp.where(lane // GROUP == f, tall, 0.0).astype(BF16)
        carried = carried + jnp.dot(toep_ref[layer, f], kept, preferred_element_type=F32)
    out_ref[...] = (mixed[0] * carried).astype(BF16)


SMEM = pl.BlockSpec(memory_space=pltpu.SMEM)
VMEM = pl.BlockSpec(memory_space=pltpu.VMEM)
HBM = pl.BlockSpec(memory_space=pltpu.HBM)


def mix(layer, core, gathered, gains, weights, taps, toep):
    def kernel(*refs):
        mix_kernel(layer, *refs)

    return pl.pallas_call(
        kernel,
        in_specs=[SMEM, VMEM, VMEM, HBM, HBM, VMEM, VMEM],
        out_specs=VMEM,
        out_shape=jax.ShapeDtypeStruct((SEQ, LANES), BF16),
        scratch_shapes=[
            pltpu.VMEM((3, SIDE, SIDE, SIDE, LANES, LANES), BF16),
            pltpu.SemaphoreType.DMA((SIDE,)),
            pltpu.VMEM((SEQ, 3 * LANES), F32),
            pltpu.VMEM((3, EXTRA + SEQ, LANES), F32),
        ],
        compiler_params=pltpu.CompilerParams(vmem_limit_bytes=VMEM_LIMIT),
        name="mix",
    )(core, gathered, gains, *weights, taps, toep)


def out_kernel(
    layer, core_ref, g_ref, own_ref, other_ref, x_ref, out_ref, held, sems, total
):
    copies = fetch(layer, core_ref, own_ref, other_ref, held, sems)
    total[...] = x_ref[...].astype(F32)
    for x in range(SIDE):
        left = jnp.concatenate(
            [g_ref[x * SIDE + y, z] for z in range(SIDE) for y in range(SIDE)], axis=1
        )
        copies[x].wait()
        right = held[x].reshape(SIDE * SIDE * LANES, LANES)
        total[...] += jnp.dot(left, right, preferred_element_type=F32)
    out_ref[...] = total[...].astype(BF16)


def project_out(layer, core, gathered, weights, activation):
    def kernel(*refs):
        out_kernel(layer, *refs)

    return pl.pallas_call(
        kernel,
        in_specs=[SMEM, VMEM, HBM, HBM, VMEM],
        out_specs=VMEM,
        out_shape=jax.ShapeDtypeStruct((SEQ, LANES), BF16),
        scratch_shapes=[
            pltpu.VMEM((SIDE, SIDE, SIDE, LANES, LANES), BF16),
            pltpu.SemaphoreType.DMA((SIDE,)),
            pltpu.VMEM((SEQ, LANES), F32),
        ],
        compiler_params=pltpu.CompilerParams(vmem_limit_bytes=VMEM_LIMIT),
        name="project_out",
    )(core, gathered, *weights, activation)


def body(tokens, embed, gain, w_in, short_filter, long_filter, skip_bias, w_out):
    core = lax.axis_index("pipe") % 2
    place_in_chip = jnp.reshape(core, (1,)).astype(jnp.int32)
    swap = [(0, 1), (1, 0), (2, 3), (3, 2)]

    own = jnp.concatenate(
        [
            short_filter[0].reshape(3 * STAPS, LANES),
            skip_bias,
            gain.astype(F32),
            jnp.zeros((1, LANES), F32),
            long_filter[0],
        ],
        axis=0,
    )
    other = hop(own, swap)
    first, second = jnp.where(core == 0, own, other), jnp.where(core == 0, other, own)
    w_in_own = w_in.reshape(3, SIDE, SIDE, SIDE, LANES, LANES)
    w_out_own = w_out.reshape(SIDE, SIDE, SIDE, LANES, LANES)
    rows = 3 * STAPS + 3
    taps = [first[:rows], second[:rows]]
    toep = toeplitz(jnp.concatenate([first[rows:], second[rows:]], axis=0))
    toep = toep.reshape(2, LANES // GROUP, SEQ, TABLE)

    ids = lax.dynamic_index_in_dim(tokens, core, 0, keepdims=False)
    one_hot = (ids[:, None] == jnp.arange(embed.shape[0], dtype=jnp.int32)[None, :]).astype(BF16)
    activation = jnp.dot(one_hot, embed, preferred_element_type=F32).astype(BF16)

    gain_rows = jnp.concatenate(
        [first[rows - 2 : rows - 1], second[rows - 2 : rows - 1], jnp.zeros((EXTRA - 2, LANES), F32)],
        axis=0,
    )
    def with_gains(activation):
        return jnp.concatenate([activation, gain_rows.astype(BF16)], axis=0)

    def layers(arrived, activation, w_in_other, w_out_other):
        gathered, gains = arrived, arrived[:, :, SEQ:]
        for layer in range(2):
            if layer > 0:
                gathered = gather_channels(activation)
            gated = mix(
                layer, place_in_chip, gathered, gains, (w_in_own, w_in_other), taps[layer], toep
            )
            activation = project_out(
                layer, place_in_chip, gather_channels(gated), (w_out_own, w_out_other), activation
            )
        return activation

    def first_chips(activation):
        block = with_gains(activation)
        others = hop(w_in_own, swap[:2]), hop(w_out_own, swap[:2])
        shape = (SIDE * SIDE, SIDE) + block.shape
        ahead = lax.cond(core == 1, gather_channels, lambda b: jnp.zeros(shape, BF16), block)
        block, ahead, *others = lax.optimization_barrier((block, ahead, *others))
        arrived = lax.cond(core == 0, lambda b, a: gather_channels(b), lambda b, a: a, block, ahead)
        return layers(arrived, activation, *others), *others

    def later_chips(activation):
        return activation, hop(w_in_own, swap[2:]), hop(w_out_own, swap[2:])

    leading = lax.axis_index("pipe") < 2
    activation, *others = lax.cond(leading, first_chips, later_chips, activation)
    activation = hop(activation, [(0, 3), (1, 2)])
    activation = lax.cond(
        leading,
        lambda a, *_: a,
        lambda a, *o: layers(gather_channels(with_gains(a)), a, *o),
        activation,
        *others,
    )

    quarters = activation.reshape(4, SEQ // 4, LANES)
    even, odd = quarters[0::2], quarters[1::2]
    keep = jnp.where(core == 0, even, odd)
    taken = hop(jnp.where(core == 0, odd, even), swap)
    row_0, row_1 = jnp.where(core == 0, taken, keep), jnp.where(core == 0, keep, taken)
    low, high = jnp.stack([row_0[0], row_1[0]]), jnp.stack([row_0[1], row_1[1]])
    passed = hop(low, [(2, 0), (3, 1)])
    return jnp.where(lax.axis_index("pipe") < 2, passed, high)


def solution(mesh):
    return jax.shard_map(
        body,
        mesh=mesh,
        in_specs=(
            P(),
            P(None, "fsdp"),
            P("pipe", "fsdp"),
            P("pipe", None, None, "fsdp"),
            P("pipe", None, None, "fsdp"),
            P("pipe", "fsdp", None),
            P("pipe", "fsdp"),
            P("pipe", None, "fsdp"),
        ),
        out_specs=P(None, "pipe", "fsdp"),
        check_vma=False,
    )
```
